256 devices in a mesh: serve: 16 (over z, core), tensor: 16 (over y, x).
Axes of the slice: x: 4, y: 4, z: 8, core: 2. Of those that a mesh axis runs over, the one named last changes fastest.
Arguments:
- hidden: bfloat16 [1024, 8192], P('serve', 'tensor'), may hold values from -6 to 6
- query_weight: bfloat16 [8192, 4096], P(None, 'tensor'), may hold values from -0.0625 to 0.0625
- adapter_down: bfloat16 [128, 8192, 64], P('serve', 'tensor'), may hold values from -0.0625 to 0.0625
- adapter_up: bfloat16 [128, 64, 4096], P('serve', None, 'tensor'), may hold values from -0.75 to 0.75
- rotated_key_cache: bfloat16 [1024, 4, 512, 128], P(('serve', 'tensor')), may hold values from -900 to 900
- cached_value_rows: bfloat16 [1024, 4, 512, 128], P(('serve', 'tensor')), may hold values from -24 to 24
- cached_length: int32 [1024], P('serve'), may hold values from 1 to 512, as said below
- request_adapter: int32 [1024], P('serve'), may hold values from 0 to 127, as said below
- group_adapters: int32 [16, 16], replicated, may hold values from -1 to 127, as said below
- adapter_pool_row: int32 [128], replicated, may hold values from 0 to 127, as said below
Outputs:
- attention: bfloat16 [1024, 4096], P(('serve', 'tensor'))
The draws below stay inside these ranges and needn't reach their ends.
Inputs may be any that keep to these rules, and one draw needn't show every extreme that they name: `request_adapter`: each request's id is a non-negative entry of its group's row of group_adapters (group = request // 64). `group_adapters`: the ids of a group are distinct; its live entries come first, then -1 entries; a group has 2 or more live entries, and some group has no -1 entry; every live entry is used by some request of the group; in every group at most 2 live ids have the same adapter_pool_row[id] // 8, and some group has exactly 2 with one such value in every draw. A permutation: adapter a is stored at row adapter_pool_row[a] of adapter_down and adapter_up. `cached_length`: some request has 512 cached positions.
All inputs are finite; a program needn't handle non-finite values.
Results may differ from the reference program's by a relative error of at most 0.02.
Values may be sent and summed in bfloat16 or wider, within the bound.
No kernel may reach another device: no remote copies, remote signals or barrier semaphores. Data moves between devices by JAX's collectives and lax.ppermute only.
A program may use at most 64 MiB of HBM per device.

```python
import math
import jax
import jax.numpy as jnp
from jax import lax

MODEL_WIDTH = 8192
HEADS = 32
KVH = 4
HD = 128
ADAPTER_RANK = 64
ROWS = 64
CACHE = 512
ADP_DEV = 8
SLOTS = 16
CAP = 2
GROUPS = 16
ROWS_ALL = 1024
ADAPTER_POOL = 128
QUERY_FEATURES = 4096


def shuffled_rows(key, count, length):

    def shuffle_one(single_key):
        return jax.random.permutation(single_key, length)
    return jax.vmap(shuffle_one)(jax.random.split(key, count))


def layout_plan(key):
    key_list = jax.random.split(key, 9)
    home_table = jax.random.permutation(key_list[0], ADAPTER_POOL).astype(jnp.int32)
    stored_adapter = jnp.argsort(home_table).astype(jnp.int32)
    forced = jax.random.randint(key_list[1], (GROUPS,), 0, GROUPS)
    values_perm = shuffled_rows(key_list[2], GROUPS, GROUPS * CAP)
    at_forced = (values_perm // CAP == forced[:, None]).astype(jnp.int32)
    ordering = jnp.argsort(at_forced, axis=1, stable=True)
    others = jnp.take_along_axis(values_perm, ordering, axis=1)[:, :SLOTS - CAP]
    first_part = forced[:, None] * CAP + jnp.arange(CAP)[None, :]
    sequence = jnp.concatenate([first_part, others], axis=1)
    sequence = jnp.take_along_axis(sequence, shuffled_rows(key_list[3], GROUPS, SLOTS), axis=1)
    home_device = sequence // CAP
    copies = sequence % CAP
    local_table = shuffled_rows(key_list[4], GROUPS * GROUPS, ADP_DEV).reshape(GROUPS, GROUPS, ADP_DEV)
    local_index = local_table[jnp.arange(GROUPS)[:, None], home_device, copies]
    adapters = stored_adapter[home_device * ADP_DEV + local_index]
    full_group = jax.random.randint(key_list[5], (), 0, GROUPS)
    live_count = jax.random.randint(key_list[6], (GROUPS,), CAP, SLOTS + 1)
    live_count = jnp.where(jnp.arange(GROUPS) == full_group, SLOTS, live_count)
    adapter_lists = jnp.where(jnp.arange(SLOTS)[None, :] < live_count[:, None], adapters, -1)
    row_ids = jnp.arange(ROWS)[None, :]
    spare_slots = jax.random.randint(key_list[7], (GROUPS, ROWS), 0, live_count[:, None])
    slot_pick = jnp.where(row_ids < live_count[:, None], row_ids, spare_slots)
    slot_pick = jnp.take_along_axis(slot_pick, shuffled_rows(key_list[8], GROUPS, ROWS), axis=1)
    request_ids = jnp.take_along_axis(adapter_lists, slot_pick, axis=1)
    return (home_table, adapter_lists.astype(jnp.int32), request_ids.reshape(-1).astype(jnp.int32))


def draw_adapter_pool_row(key, part):
    return layout_plan(key)[0]


def draw_group_adapters(key, part):
    return layout_plan(key)[1]


def draw_request_adapter(key, part):
    return layout_plan(key)[2]


def draw_cached_length(key, part):
    key = jax.random.fold_in(key, 21)
    key_list = jax.random.split(key, 3)
    ceiling = jax.random.randint(key_list[0], (GROUPS, 1), max(CACHE // 8, 1), CACHE + 1)
    raw_lengths = jax.random.randint(key_list[1], (GROUPS, ROWS), 1, CACHE + 1)
    lengths = jnp.minimum(raw_lengths, ceiling).reshape(-1)
    chosen_row = jax.random.randint(key_list[2], (), 0, GROUPS * ROWS)
    lengths = jnp.where(jnp.arange(GROUPS * ROWS) == chosen_row, CACHE, lengths)
    return lengths.astype(jnp.int32)


def draw_rotated_key_cache(key, part):
    key = jax.random.fold_in(key, 22)
    key_list = jax.random.split(key, 1)
    array_shape = (ROWS_ALL, KVH, CACHE, HD)
    values = jnp.clip(jax.random.normal(key_list[0], array_shape, jnp.float32), -6.0, 6.0)
    return values.astype(jnp.bfloat16)


def levels(key, dims, pieces, smallest, largest):
    def one(axis_at, shards_of):
        steps = jax.random.uniform(jax.random.fold_in(jax.random.fold_in(key, 6), axis_at), (shards_of,), jnp.float32, smallest / len(pieces), largest / len(pieces))
        return jnp.repeat(jnp.exp(steps), dims[axis_at] // shards_of).reshape((-1,) + (1,) * (len(dims) - axis_at - 1))

    level = one(*pieces[0])
    for cut in pieces[1:]:
        level = level * one(*cut)
    return level


def scatter_about(rng, extent, spread, limit, pieces=(), kind=jnp.bfloat16):
    drawn = spread * jax.random.normal(rng, extent, jnp.float32)
    if pieces:
        drawn = drawn * levels(rng, extent, pieces, -0.22, 0.18)
    return jnp.clip(drawn, -limit, limit).astype(kind)


def setup_inputs(seed: int = 0) -> dict:
    seeds = jax.random.split(jax.random.key(seed), 11)
    return {
        "hidden": scatter_about(seeds[0], (ROWS_ALL, MODEL_WIDTH), 1.0, 6.0, ((0, 16), (1, 16))),
        "query_weight": scatter_about(seeds[1], (MODEL_WIDTH, QUERY_FEATURES), MODEL_WIDTH ** -0.5, 0.0625, ((1, 16),)),
        "adapter_down": scatter_about(seeds[2], (ADAPTER_POOL, MODEL_WIDTH, ADAPTER_RANK), MODEL_WIDTH ** -0.5, 0.0625, ((0, 16), (1, 16))),
        "adapter_up": scatter_about(seeds[3], (ADAPTER_POOL, ADAPTER_RANK, QUERY_FEATURES), ADAPTER_RANK ** -0.5, 0.75, ((0, 16), (2, 16))),
        "rotated_key_cache": draw_rotated_key_cache(jax.random.fold_in(seeds[10], 71), 0),
        "cached_value_rows": scatter_about(seeds[5], (ROWS_ALL, KVH, CACHE, HD), 4.0, 24.0, ((0, 256),)),
        "cached_length": draw_cached_length(jax.random.fold_in(seeds[10], 71), 0),
        "request_adapter": draw_request_adapter(jax.random.fold_in(seeds[10], 71), 0),
        "group_adapters": draw_group_adapters(jax.random.fold_in(seeds[10], 71), 0),
        "adapter_pool_row": draw_adapter_pool_row(jax.random.fold_in(seeds[10], 71), 0),
    }


ADAPTER_SCALE = 0.5
ROPE_BASE = 500000.0
NEG_LARGE = -1.0e30


def rotate_query(query_heads, positions):
    half_width = query_heads.shape[-1] // 2
    exponent = jnp.arange(half_width, dtype=jnp.float32) * (2.0 / query_heads.shape[-1])
    inverse = jnp.exp(-math.log(ROPE_BASE) * exponent)
    angles = positions.astype(jnp.float32)[:, None] * inverse[None, :]
    cosine = jnp.cos(angles)[:, None, :]
    sine_part = jnp.sin(angles)[:, None, :]
    first_half = query_heads[..., :half_width]
    second_half = query_heads[..., half_width:]
    return jnp.concatenate([first_half * cosine - second_half * sine_part, second_half * cosine + first_half * sine_part], axis=-1)


def reference(hidden, query_weight, adapter_down, adapter_up, rotated_key_cache, cached_value_rows, cached_length, request_adapter, group_adapters, adapter_pool_row):
    def project_group(operands):
        rows_in, adapters_in, list_in = operands
        pool_row_count = jnp.take(adapter_pool_row, jnp.maximum(list_in, 0), axis=0)
        down_pool_rows = jnp.take(adapter_down, pool_row_count, axis=0).astype(jnp.float32)
        up_pool_rows = jnp.take(adapter_up, pool_row_count, axis=0).astype(jnp.float32)
        row_slot = ((adapters_in[:, None] == list_in[None, :]) & (list_in[None, :] >= 0)).astype(jnp.float32)
        partial_value = jnp.einsum("rd,sdk->rsk", rows_in.astype(jnp.float32), down_pool_rows)
        shrunk = jnp.einsum("rs,rsk->rk", row_slot, partial_value).astype(jnp.bfloat16)
        wide_shrunk = (row_slot[:, :, None] * shrunk.astype(jnp.float32)[:, None, :]).reshape(ROWS, SLOTS * ADAPTER_RANK)
        widen_back = jnp.dot(wide_shrunk, up_pool_rows.reshape(SLOTS * ADAPTER_RANK, QUERY_FEATURES))
        base_product = jnp.dot(rows_in, query_weight, preferred_element_type=jnp.float32)
        return base_product + ADAPTER_SCALE * widen_back

    query_linear = lax.map(project_group, (hidden.reshape(GROUPS, ROWS, MODEL_WIDTH), request_adapter.reshape(GROUPS, ROWS), group_adapters))
    query_rows = rotate_query(query_linear.reshape(ROWS_ALL, HEADS, HD), cached_length).astype(jnp.bfloat16)

    def attend_group(operands):
        query_in, keys_in, values_in, lengths_in = operands
        grouped = query_in.reshape(ROWS, KVH, HEADS // KVH, HD).astype(jnp.float32)
        scores = jnp.einsum("rkgd,rktd->rkgt", grouped, keys_in.astype(jnp.float32)) * (HD ** -0.5)
        valid_mask = (jnp.arange(CACHE)[None, :] < lengths_in[:, None])[:, None, None, :]
        row_max = jnp.max(jnp.where(valid_mask, scores, NEG_LARGE), axis=3, keepdims=True)
        weights = jnp.where(valid_mask, jnp.exp(scores - row_max), 0.0).astype(jnp.bfloat16)
        totals = jnp.sum(weights.astype(jnp.float32), axis=3)
        numerator = jnp.einsum("rkgt,rktd->rkgd", weights.astype(jnp.float32), values_in.astype(jnp.float32))
        return (numerator / totals[..., None]).reshape(ROWS, QUERY_FEATURES).astype(jnp.bfloat16)

    outcome = lax.map(attend_group, (query_rows.reshape(GROUPS, ROWS, HEADS, HD), rotated_key_cache.reshape(GROUPS, ROWS, KVH, CACHE, HD), cached_value_rows.reshape(GROUPS, ROWS, KVH, CACHE, HD), cached_length.reshape(GROUPS, ROWS)))
    return outcome.reshape(ROWS_ALL, QUERY_FEATURES)
```

```python
import functools
import math

import jax
import jax.numpy as jnp
from jax import lax
from jax.experimental import pallas as pl
from jax.experimental.pallas import tpu as pltpu
from jax.sharding import PartitionSpec as P

ADAPTER_SCALE = 0.5
ROPE_BASE = 500000.0
NEG_LARGE = -1e30
BF = jnp.bfloat16
F32 = jnp.float32
CORES = 2
SLOTS_PER_CHIP = 4


def vmem_specs(count):
    return [pl.BlockSpec(memory_space=pltpu.VMEM) for _ in range(count)]


def lane(shape):
    return lax.broadcasted_iota(jnp.int32, shape, len(shape) - 1)


def pack_down_kernel(down_ref, out_ref):
    for pair in range(down_ref.shape[0] // 2):
        out_ref[:, pair * 128 : pair * 128 + 128] = jnp.concatenate(
            [down_ref[2 * pair], down_ref[2 * pair + 1]], axis=1
        )


def pack_down(adapter_down):
    count, depth, rank = adapter_down.shape
    return pl.pallas_call(
        pack_down_kernel,
        out_shape=jax.ShapeDtypeStruct((depth, count * rank), BF),
        in_specs=vmem_specs(1),
        out_specs=vmem_specs(1)[0],
    )(adapter_down)


def home_kernel(first_ref, source_ref, message_ref, own_down, other_down, own_up, other_up, out_ref):
    depth = own_down.shape[0]
    rows = message_ref.shape[0]
    hidden = message_ref[:, :depth]
    wanted = message_ref[:, depth:].astype(F32)
    half = (lane((rows, 128)) >= 64).astype(F32)
    total = jnp.zeros((rows, 128), F32)
    for side, down in enumerate((own_down, other_down)):
        product = jnp.dot(hidden, down[...], preferred_element_type=F32)
        first = first_ref[side].astype(F32)
        for pair in range(product.shape[1] // 128):
            here = wanted == first + (2.0 * pair) + half
            total += jnp.where(here, product[:, pair * 128 : pair * 128 + 128], 0.0)
    total = total + pltpu.roll(total, 64, 1)
    high = total.astype(BF).astype(F32)
    low = (total - high).astype(BF).astype(F32)
    both = jnp.where(half > 0.5, low, high).astype(BF)
    out_ref[:32, :128] = both[:32]
    out_ref[:32, 128:] = both[32:]
    for slot in range(SLOTS_PER_CHIP):
        source = source_ref[slot]
        at = 32 + 64 * slot

        @pl.when(source < 8)
        def _():
            out_ref[at : at + 64, :] = own_up[jnp.minimum(source, 7)]

        @pl.when(source >= 8)
        def _():
            out_ref[at : at + 64, :] = other_up[jnp.maximum(source - 8, 0)]


def home_step(first, source, message, own_down, other_down, own_up, other_up):
    return pl.pallas_call(
        home_kernel,
        out_shape=jax.ShapeDtypeStruct((32 + 64 * SLOTS_PER_CHIP, 256), BF),
        in_specs=[pl.BlockSpec(memory_space=pltpu.SMEM)] * 2 + vmem_specs(5),
        out_specs=vmem_specs(1)[0],
    )(first, source, message, own_down, other_down, own_up, other_up)


def collect_kernel(*refs):
    out_ref = refs[-1]
    total = refs[0][:32, :].astype(F32)
    for ref in refs[1:-1]:
        total += ref[:32, :].astype(F32)
    total = total.astype(BF)
    for place in range(out_ref.shape[0]):
        out_ref[place] = total


def collect(replies, copies):
    return pl.pallas_call(
        collect_kernel,
        out_shape=jax.ShapeDtypeStruct((copies, 32, 256), BF),
        in_specs=vmem_specs(len(replies)),
        out_specs=vmem_specs(1)[0],
    )(*replies)


def base_kernel(hidden_ref, weight_ref, out_ref):
    @pl.when(pl.program_id(0) == 0)
    def _():
        out_ref[...] = jnp.zeros_like(out_ref)

    out_ref[...] += jnp.dot(hidden_ref[0], weight_ref[...], preferred_element_type=F32)


def base_product(hidden_all, weight):
    parts, rows, depth = hidden_all.shape
    columns = weight.shape[1]
    return pl.pallas_call(
        base_kernel,
        grid=(parts,),
        out_shape=jax.ShapeDtypeStruct((rows, columns), F32),
        in_specs=[
            pl.BlockSpec((1, rows, depth), lambda i: (i, 0, 0)),
            pl.BlockSpec((depth, columns), lambda i: (i, 0)),
        ],
        out_specs=pl.BlockSpec((rows, columns), lambda i: (0, 0)),
    )(hidden_all, weight)


def finish_kernel(partial_ref, table_ref, wanted_ref, base_ref, cos_ref, sin_ref, *refs):
    out_ref = refs[-1]
    replies = refs[:-1]
    total = partial_ref[0].astype(F32)
    for place in range(1, partial_ref.shape[0]):
        total += partial_ref[place].astype(F32)
    total = jnp.concatenate([total[:, :128], total[:, 128:]], axis=0)
    shrunk = (total + pltpu.roll(total, 64, 1)).astype(BF).astype(F32)
    shrunk = jnp.concatenate([shrunk, shrunk], axis=1)
    wanted = wanted_ref[...]
    query = jnp.zeros(base_ref.shape, F32)
    for place, reply in enumerate(replies):
        here = wanted == table_ref[place : place + 1, :]
        wide = jnp.where(here, shrunk, 0.0).astype(BF)
        query += jnp.dot(wide, reply[32:, :], preferred_element_type=F32)
    query = base_ref[...] + ADAPTER_SCALE * query
    for head in range(query.shape[1] // 128):
        piece = query[:, head * 128 : head * 128 + 128]
        turned = piece * cos_ref[...] + pltpu.roll(piece, 64, 1) * sin_ref[...]
        out_ref[:, head * 128 : head * 128 + 128] = turned.astype(BF)


def finish(partials, table, wanted, base, cosine, sine, replies):
    return pl.pallas_call(
        finish_kernel,
        out_shape=jax.ShapeDtypeStruct(base.shape, BF),
        in_specs=vmem_specs(6 + len(replies)),
        out_specs=vmem_specs(1)[0],
    )(partials, table, wanted, base, cosine, sine, *replies)


def rotation(positions, head_dim):
    half_width = head_dim // 2
    exponent = jnp.arange(half_width, dtype=F32) * (2.0 / head_dim)
    inverse = jnp.exp(-math.log(ROPE_BASE) * exponent)
    angles = positions.astype(F32)[:, None] * inverse[None, :]
    cosine, sine = jnp.cos(angles), jnp.sin(angles)
    return (
        jnp.concatenate([cosine, cosine], axis=1),
        jnp.concatenate([-sine, sine], axis=1),
    )


def attend_rows(row_query, rotated_key_cache, cached_value_rows, lengths):
    local_rows, kv_heads, cache_count, head_dim = rotated_key_cache.shape
    grouped = row_query.reshape(local_rows, kv_heads, -1, head_dim)
    scores = jnp.einsum(
        "rkgd,rktd->rkgt", grouped, rotated_key_cache, preferred_element_type=F32
    ) * head_dim ** (-0.5)
    valid_mask = (jnp.arange(cache_count)[None, :] < lengths[:, None])[:, None, None, :]
    row_max = jnp.max(jnp.where(valid_mask, scores, NEG_LARGE), axis=3, keepdims=True)
    weights = jnp.where(valid_mask, jnp.exp(scores - row_max), 0.0).astype(BF)
    totals = jnp.sum(weights.astype(F32), axis=3)
    numerator = jnp.einsum(
        "rkgt,rktd->rkgd", weights, cached_value_rows, preferred_element_type=F32
    )
    return (numerator / totals[..., None]).reshape(local_rows, -1).astype(BF)


def slot_table(group_adapters, adapter_pool_row, chips):
    live = group_adapters >= 0
    ids = jnp.arange(adapter_pool_row.shape[0], dtype=jnp.int32)
    rows = jnp.sum(
        jnp.where(group_adapters[:, :, None] == ids, adapter_pool_row[None, None, :], 0), axis=2
    )
    chip = jnp.where(live, rows // 16, -1)
    count = group_adapters.shape[1]
    earlier = jnp.arange(count)[None, :] < jnp.arange(count)[:, None]
    rank = jnp.sum(
        jnp.where((chip[:, :, None] == chip[:, None, :]) & earlier[None], 1, 0), axis=2
    )
    here = (chip[:, None, None, :] == jnp.arange(chips)[None, :, None, None]) & (
        rank[:, None, None, :] == jnp.arange(SLOTS_PER_CHIP)[None, None, :, None]
    )
    return jnp.sum(jnp.where(here, rows[:, None, None, :] + 1, 0), axis=3) - 1


def on_device(
    hidden,
    query_weight,
    adapter_down,
    adapter_up,
    rotated_key_cache,
    cached_value_rows,
    cached_length,
    request_adapter,
    group_adapters,
    adapter_pool_row,
):
    group = lax.axis_index("serve")
    tensor_index = lax.axis_index("tensor")
    serve_size = lax.axis_size("serve")
    tensor_size = lax.axis_size("tensor")
    chips = serve_size // CORES
    chip, core = group // CORES, group % CORES
    rows = hidden.shape[0]
    head_dim = rotated_key_cache.shape[3]
    local_rows = rotated_key_cache.shape[0]

    def along(array, steps):
        return lax.ppermute(
            array,
            "serve",
            [(i, (i // 2 + steps) % chips * 2 + i % 2) for i in range(serve_size)],
        )

    def other_core(array):
        return lax.ppermute(array, "serve", [(i, i ^ 1) for i in range(serve_size)])

    ids = jnp.arange(adapter_pool_row.shape[0], dtype=jnp.int32)
    wanted = jnp.sum(
        jnp.where(request_adapter[:, None] == ids, adapter_pool_row[None, :], 0), axis=1
    )
    message = jnp.concatenate(
        [hidden, jnp.broadcast_to(wanted.astype(BF)[:, None], (rows, 128))], axis=1
    )
    own_down = pack_down(adapter_down)
    other_down = other_core(own_down)
    other_up = other_core(adapter_up)
    hidden_all = lax.all_to_all(
        jnp.broadcast_to(hidden[None], (tensor_size,) + hidden.shape), "tensor", 0, 0
    )
    arrived = [message] + [along(message, d) for d in range(1, chips)]

    table = slot_table(group_adapters, adapter_pool_row, chips)
    distance = jnp.arange(chips)
    asking = (chip - distance) % chips * CORES + core
    answering = (chip + distance) % chips
    by_chip = jnp.sum(
        jnp.where((distance == chip)[None, :, None], table, 0), axis=1
    )
    source = jnp.sum(
        jnp.where(
            (asking[:, None] == jnp.arange(serve_size)[None, :])[:, :, None], by_chip[None], 0
        ),
        axis=1,
    )
    source = jnp.maximum(source, 0)
    source = (source % 8) + 8 * ((source // 8 % 2) ^ core)
    my_table = lax.dynamic_index_in_dim(table, group, 0, keepdims=False)
    my_table = jnp.sum(
        jnp.where((answering[:, None] == distance[None, :])[:, :, None], my_table[None], 0), axis=1
    )
    my_table = jnp.repeat(my_table.astype(F32), 64, axis=1)
    first = jnp.stack([group * 8, (group ^ 1) * 8]).astype(jnp.int32)

    replies = []
    for d in range(chips):
        reply = home_step(
            first, source[d], arrived[d], own_down, other_down, adapter_up, other_up
        )
        replies.append(along(reply, -d) if d else reply)
    partials = lax.all_to_all(collect(replies, tensor_size), "tensor", 0, 0)
    base = base_product(hidden_all, query_weight)
    cosine, sine = rotation(cached_length, head_dim)
    wanted_wide = jnp.broadcast_to(wanted.astype(F32)[:, None], (rows, 256))
    query_rows = finish(partials, my_table, wanted_wide, base, cosine, sine, replies)
    row_query = lax.all_to_all(query_rows, "tensor", split_axis=0, concat_axis=1, tiled=True)
    lengths = lax.dynamic_slice_in_dim(cached_length, tensor_index * local_rows, local_rows, 0)
    return attend_rows(row_query, rotated_key_cache, cached_value_rows, lengths)


def solution(mesh):
    placed = (
        P("serve", "tensor"),
        P(None, "tensor"),
        P("serve", "tensor", None),
        P("serve", None, "tensor"),
        P(("serve", "tensor"), None, None, None),
        P(("serve", "tensor"), None, None, None),
        P("serve"),
        P("serve"),
        P(),
        P(),
    )
    return jax.shard_map(
        on_device,
        mesh=mesh,
        in_specs=placed,
        out_specs=P(("serve", "tensor"), None),
        check_vma=False,
    )
```
